512 devices in a mesh: tenant: 16 (over y, x_lo), fsdp: 32 (over x_hi, z, core).
Axes of the slice: x: 4 (x_hi: 2, x_lo: 2; x = x_hi * 2 + x_lo), y: 8, z: 8, core: 2. Of those that a mesh axis runs over, the one named last changes fastest.
Arguments:
- encoded: bfloat16 [3072, 3200], P(('tenant', 'fsdp')), may hold values from -6 to 6
- encoder_norm_gain: bfloat16 [3200], replicated, may hold values from 0.099609375 to 1.8984375
- encoder_projection_weight: bfloat16 [3200, 8192], P(None, 'fsdp'), may hold values from -0.109375 to 0.109375
- frozen_value_weight: bfloat16 [8192, 1024], P('fsdp'), may hold values from -0.0625 to 0.0625
- tenant_down_weight: bfloat16 [16, 8192, 64], P('tenant', 'fsdp'), may hold values from -0.0625 to 0.0625
- tenant_up_weight: bfloat16 [16, 64, 1024], P('tenant'), may hold values from -0.75 to 0.75
- embedded_text_rows: bfloat16 [16, 1024, 8192], P('tenant', None, 'fsdp'), may hold values from -6 to 6
- image_row_index: int32 [16, 3072], P('tenant'), may hold values from 0 to 3071, as said below
- targets: bfloat16 [16, 4096, 1024], P('tenant', 'fsdp'), may hold values from -6 to 6
- row_loss_mask: int32 [16, 4096], P('tenant', 'fsdp'), may hold values 0 or 1
Outputs:
- values: bfloat16 [16, 4096, 1024], P('tenant', 'fsdp')
- down_gradient: float32 [16, 8192, 64], P('tenant', 'fsdp')
- up_matrix_gradient: float32 [16, 64, 1024], P('tenant', None, 'fsdp')
- text_row_gradient: bfloat16 [16, 1024, 8192], P('tenant', None, 'fsdp')
The draws below stay inside these ranges and needn't reach their ends.
Inputs may be any that keep to these rules, and one draw needn't show every extreme that they name: For every tenant, the 96 image positions of block b hold, in some order, exactly the image rows g * 32 * 6 + b * 6 + v for every g < 16 and v < 6; each tenant's image_row_index is thus a permutation of the image rows.
All inputs are finite; a program needn't handle non-finite values. No bound on the sum of `row_loss_mask` on one device may be relied on, other than what follows from the above.
Results may differ from the reference program's by a relative error of at most 0.025.
Values may be sent and summed in bfloat16 or wider, within the bound.
No kernel may reach another device: no remote copies, remote signals or barrier semaphores. Data moves between devices by JAX's collectives and lax.ppermute only.
A program may use at most 64 MiB of HBM per device.

```python
import jax
import jax.numpy as jnp
from jax import lax

MODEL_WIDTH = 8192
VALUE_WIDTH = 1024
EW = 3200
ADAPTER_RANK = 64
VIS_DEV = 6
TXT_DEV = 32
VIS_ALL = 3072
TEXT_LEN = 1024
SEQ = 4096
N_TENANT = 16
N_FSDP = 32


def block_order(one_key):
    return jax.random.permutation(one_key, VIS_DEV * N_TENANT)


def draw_image_row_index(key, part):
    key = jax.random.fold_in(key, 7)
    keys = jax.random.split(key, N_TENANT * N_FSDP)
    orders = jax.vmap(block_order)(keys).astype(jnp.int32)
    group_of = orders // VIS_DEV
    slot_of = orders % VIS_DEV
    block_of = (jnp.arange(N_TENANT * N_FSDP, dtype=jnp.int32) % N_FSDP)[:, None]
    rows = group_of * (N_FSDP * VIS_DEV) + block_of * VIS_DEV + slot_of
    return rows.reshape(N_TENANT, VIS_ALL).astype(jnp.int32)


def touch_ends(drawn, rng, smallest, top_value):
    shape = drawn.shape
    spot = [jax.random.randint(jax.random.fold_in(rng, axis), (), 0, shape[axis]) for axis in range(len(shape))]
    drawn = drawn.at[tuple(spot)].set(smallest)
    longest = shape.index(max(shape))
    spot[longest] = (spot[longest] + 1) % shape[longest]
    return drawn.at[tuple(spot)].set(top_value)


def block_scale(stream_key, extent, cuts, low, high):
    loudness = 1.0
    for axis_at, parts in cuts:
        draws = jax.random.uniform(jax.random.fold_in(jax.random.fold_in(stream_key, 6), axis_at), (parts,), jnp.float32, low / len(cuts), high / len(cuts))
        loudness = loudness * jnp.repeat(jnp.exp(draws), extent[axis_at] // parts).reshape((-1,) + (1,) * (len(extent) - 1 - axis_at))
    return loudness


def normal_values(stream_key, extent, scale, bound, shards=(), kind=jnp.bfloat16):
    loudness = block_scale(stream_key, extent, shards, -0.22, 0.18) if shards else 1.0
    drawn = jax.random.normal(stream_key, extent, jnp.float32) * scale * loudness
    return jnp.minimum(jnp.maximum(drawn, -bound), bound).astype(kind)


def setup_inputs(seed: int = 0) -> dict:
    key_of = jax.random.split(jax.random.key(seed), 11)
    return {
        "encoded": normal_values(key_of[0], (VIS_ALL, EW), 1.0, 6.0, ((0, 512),)),
        "encoder_norm_gain": jnp.clip(1.0 + 0.18 * jax.random.normal(key_of[1], (EW,), jnp.float32), 0.099609375, 1.8984375).astype(jnp.bfloat16),
        "encoder_projection_weight": normal_values(key_of[2], (EW, MODEL_WIDTH), EW ** -0.5, 0.109375, ((1, 32),)),
        "frozen_value_weight": normal_values(key_of[3], (MODEL_WIDTH, VALUE_WIDTH), MODEL_WIDTH ** -0.5, 0.0625, ((0, 32),)),
        "tenant_down_weight": normal_values(key_of[4], (N_TENANT, MODEL_WIDTH, ADAPTER_RANK), MODEL_WIDTH ** -0.5, 0.0625, ((0, 16), (1, 32))),
        "tenant_up_weight": normal_values(key_of[5], (N_TENANT, ADAPTER_RANK, VALUE_WIDTH), ADAPTER_RANK ** -0.5, 0.75, ((0, 16),)),
        "embedded_text_rows": normal_values(key_of[6], (N_TENANT, TEXT_LEN, MODEL_WIDTH), 1.0, 6.0, ((0, 16), (2, 32))),
        "image_row_index": draw_image_row_index(jax.random.fold_in(key_of[10], 71), 0),
        "targets": normal_values(key_of[8], (N_TENANT, SEQ, VALUE_WIDTH), 1.0, 6.0, ((0, 16), (1, 32))),
        "row_loss_mask": touch_ends((jax.random.randint(key_of[9], (N_TENANT, SEQ), 0, 2) < 1).astype(jnp.int32), jax.random.fold_in(key_of[9], 1), 0, 1),
    }


ADAPTER_SCALE = 0.5

def sliced_sum(rows_in, weight):
    width = MODEL_WIDTH // N_FSDP

    def step(running, index):
        first = index * width
        left_part = lax.dynamic_slice_in_dim(rows_in, first, width, 1)
        right_part = lax.dynamic_slice_in_dim(weight, first, width, 0)
        term = jnp.dot(left_part, right_part, preferred_element_type=jnp.float32).astype(jnp.bfloat16)
        term = lax.optimization_barrier(term)
        return (running + term.astype(jnp.float32), None)
    start_sum = jnp.zeros((rows_in.shape[0], weight.shape[1]), jnp.float32)
    result, _ = lax.scan(step, start_sum, jnp.arange(N_FSDP, dtype=jnp.int32))
    return result

def reference(encoded, encoder_norm_gain, encoder_projection_weight, frozen_value_weight, tenant_down_weight, tenant_up_weight, embedded_text_rows, image_row_index, targets, row_loss_mask):
    features = encoded.astype(jnp.float32)
    average = lax.optimization_barrier(jnp.mean(features, axis=-1, keepdims=True))
    centred = features - average
    spread = lax.optimization_barrier(jnp.mean(centred * centred, axis=-1, keepdims=True))
    normed = (centred * lax.rsqrt(spread + 1e-06) * encoder_norm_gain.astype(jnp.float32)).astype(jnp.bfloat16)
    visual = jax.nn.gelu(jnp.dot(normed, encoder_projection_weight, preferred_element_type=jnp.float32)).astype(jnp.bfloat16)
    shared = sliced_sum(visual, frozen_value_weight)
    vis_block = VIS_DEV * N_TENANT
    block_rows = vis_block + TXT_DEV

    def tenant_update(inputs):
        tenant_down_matrix, tenant_up_matrix, text_local, mapping, target_rows, mask_rows = inputs
        text_frozen = sliced_sum(text_local, frozen_value_weight)
        placed = jnp.take(visual, mapping, axis=0)
        tenant_sequence = jnp.concatenate((placed.reshape(N_FSDP, vis_block, MODEL_WIDTH), text_local.reshape(N_FSDP, TXT_DEV, MODEL_WIDTH)), axis=1).reshape(SEQ, MODEL_WIDTH)
        frozen_all = jnp.concatenate((jnp.take(shared, mapping, axis=0).reshape(N_FSDP, vis_block, VALUE_WIDTH), text_frozen.reshape(N_FSDP, TXT_DEV, VALUE_WIDTH)), axis=1).reshape(SEQ, VALUE_WIDTH)
        frozen_output = frozen_all.astype(jnp.bfloat16)
        low_rank_output = sliced_sum(tenant_sequence, tenant_down_matrix).astype(jnp.bfloat16)
        mixed_sequence = frozen_output.astype(jnp.float32) + ADAPTER_SCALE * jnp.dot(low_rank_output, tenant_up_matrix, preferred_element_type=jnp.float32)
        values_out = mixed_sequence.astype(jnp.bfloat16)
        weight_mask = mask_rows.astype(jnp.float32)[:, None]
        output_cotangent = (weight_mask * (values_out.astype(jnp.float32) - target_rows.astype(jnp.float32)) * 0.25).astype(jnp.bfloat16)
        up_gradient_result = ADAPTER_SCALE * jnp.dot(low_rank_output.T, output_cotangent, preferred_element_type=jnp.float32)
        backward_low_rank = jnp.dot(output_cotangent, tenant_up_matrix.T, preferred_element_type=jnp.float32).astype(jnp.bfloat16)
        down_gradient_result = ADAPTER_SCALE * jnp.dot(tenant_sequence.T, backward_low_rank, preferred_element_type=jnp.float32)
        text_cotangent = output_cotangent.reshape(N_FSDP, block_rows, VALUE_WIDTH)[:, vis_block:].reshape(TEXT_LEN, VALUE_WIDTH)
        backward_text = backward_low_rank.reshape(N_FSDP, block_rows, ADAPTER_RANK)[:, vis_block:].reshape(TEXT_LEN, ADAPTER_RANK)
        text_result = jnp.dot(text_cotangent, frozen_value_weight.T, preferred_element_type=jnp.float32) + ADAPTER_SCALE * jnp.dot(backward_text, tenant_down_matrix.T, preferred_element_type=jnp.float32)
        return (values_out, down_gradient_result, up_gradient_result, text_result.astype(jnp.bfloat16))
    values, down_gradient, up_matrix_gradient, text_row_gradient = lax.map(tenant_update, (tenant_down_weight, tenant_up_weight, embedded_text_rows, image_row_index, targets, row_loss_mask))
    return (values, down_gradient, up_matrix_gradient, text_row_gradient)
```

```python
import jax
import jax.numpy as jnp
from jax import lax
from jax.sharding import Mesh, PartitionSpec as P

ADAPTER_SCALE = 0.5
TENANT = ("y", "x_lo")
CHIPS = ("x_hi", "z")
FSDP = ("x_hi", "z", "core")
N_CHIP = 16
N_TENANT = 16
PAD = 8


def swap(block):
    return lax.ppermute(block, "core", [(0, 1), (1, 0)])


def exchange(block, axes):
    return lax.all_to_all(block, axes, 0, 0, tiled=True)


def share(block, axes, count):
    return exchange(jnp.broadcast_to(block[None], (count,) + block.shape), axes)


def dot(a, b):
    return jnp.dot(a, b, preferred_element_type=jnp.float32)


def dot_t(a, b):
    return lax.dot_general(a, b, (((1,), (1,)), ((), ())), preferred_element_type=jnp.float32)


def t_dot(a, b):
    return lax.dot_general(a, b, (((0,), (0,)), ((), ())), preferred_element_type=jnp.float32)


def body(
    encoded,
    encoder_norm_gain,
    encoder_projection_weight,
    frozen_value_weight,
    tenant_down_weight,
    tenant_up_weight,
    embedded_text_rows,
    image_row_index,
    targets,
    row_loss_mask,
):
    bf16, f32 = jnp.bfloat16, jnp.float32
    core = lax.axis_index("core")
    device_row = lax.axis_index(FSDP)
    down = tenant_down_weight[0]
    up = tenant_up_weight[0]
    text = embedded_text_rows[0]
    vis_dev = encoded.shape[0]
    width = text.shape[1]
    value_width = frozen_value_weight.shape[1]
    rank = down.shape[1]
    block_rows = targets.shape[1]
    text_block = text.shape[0] // (2 * N_CHIP)
    vis_block = block_rows - text_block

    features = encoded.astype(f32)
    centred = features - jnp.mean(features, axis=-1, keepdims=True)
    spread = jnp.mean(centred * centred, axis=-1, keepdims=True)
    normed = (centred * lax.rsqrt(spread + 1e-06) * encoder_norm_gain.astype(f32)).astype(bf16)
    normed = jnp.pad(normed, ((0, PAD - vis_dev), (0, 0)))
    normed_rows = share(normed, CHIPS, N_CHIP).reshape(N_CHIP * PAD, -1)

    text_cut = text.reshape(N_CHIP, 2, text_block, width)
    text_own = lax.dynamic_index_in_dim(text_cut, core, 1, False).reshape(-1, width)
    text_send = lax.dynamic_index_in_dim(text_cut, 1 - core, 1, False).reshape(-1, width)
    text_other = swap(text_send)
    mixed_own = jnp.concatenate((frozen_value_weight, down), axis=1)
    mixed_other = swap(mixed_own)
    projection_other = swap(encoder_projection_weight)
    all_down = share(down, TENANT, N_TENANT)
    all_down_own = all_down.transpose(1, 0, 2).reshape(width, N_TENANT * rank)
    all_down_other = swap(all_down_own)

    text_part = (dot(text_own, mixed_own) + dot(text_other, mixed_other)).astype(bf16)
    text_parts = exchange(text_part.reshape(N_CHIP, text_block, value_width + rank), CHIPS)
    text_sum = jnp.sum(text_parts.astype(f32), axis=0).astype(bf16)

    visual_own = jax.nn.gelu(dot(normed_rows, encoder_projection_weight)).astype(bf16)
    visual_other = jax.nn.gelu(dot(normed_rows, projection_other)).astype(bf16)
    wide_own = jnp.concatenate((frozen_value_weight, all_down_own), axis=1)
    wide_other = jnp.concatenate((mixed_other[:, :value_width], all_down_other), axis=1)
    image_part = (dot(visual_own, wide_own) + dot(visual_other, wide_other)).astype(bf16)
    image_parts = exchange(image_part.reshape(N_CHIP, PAD, -1), CHIPS)
    image_sum = jnp.sum(image_parts.astype(f32), axis=0).astype(bf16)
    image_low = image_sum[:, value_width:].reshape(PAD, N_TENANT, rank).transpose(1, 0, 2)
    image_frozen = jnp.broadcast_to(image_sum[None, :, :value_width], (N_TENANT, PAD, value_width))
    image_rows = exchange(jnp.concatenate((image_frozen, image_low), axis=2), TENANT)
    visual_all = share(jnp.concatenate((visual_own, visual_other), axis=1), TENANT, N_TENANT)

    place = lax.dynamic_slice_in_dim(image_row_index[0], device_row * vis_block, vis_block, 0)
    group = place // (2 * N_CHIP * vis_dev)
    slot = place - group * (2 * N_CHIP * vis_dev) - device_row * vis_dev
    order = (group * PAD + slot)[:, None] == jnp.arange(N_TENANT * PAD, dtype=jnp.int32)[None]
    order = order.astype(bf16)
    image_rows = image_rows.reshape(N_TENANT * PAD, value_width + rank)
    picked = dot(order, image_rows).astype(bf16)

    def rows_of(block, wanted, mask):
        frozen, low = block[:, :value_width], block[:, value_width:]
        mixed = frozen.astype(f32) + ADAPTER_SCALE * dot(low, up)
        values = mixed.astype(bf16)
        weight = mask.astype(f32)[:, None]
        cotangent = (weight * (values.astype(f32) - wanted.astype(f32)) * 0.25).astype(bf16)
        back = (ADAPTER_SCALE * dot_t(cotangent, up).astype(bf16).astype(f32)).astype(bf16)
        return low, values, cotangent, back

    wanted, mask = targets[0], row_loss_mask[0]
    text_low, text_values, text_cot, text_back = rows_of(
        text_sum, wanted[vis_block:], mask[vis_block:]
    )
    image_low, image_values, image_cot, image_back = rows_of(
        picked, wanted[:vis_block], mask[:vis_block]
    )
    values = jnp.concatenate((image_values, text_values), axis=0)

    text_back_rows = share(jnp.concatenate((text_cot, text_back), axis=1), CHIPS, N_CHIP)
    text_back_rows = text_back_rows.reshape(N_CHIP * text_block, value_width + rank)
    text_grad_own = dot_t(text_back_rows, mixed_own).astype(bf16)
    text_grad_send = dot_t(text_back_rows, mixed_other).astype(bf16)
    text_grad_other = swap(text_grad_send)
    own_cut = text_grad_own.reshape(N_CHIP, 1, text_block, width)
    other_cut = text_grad_other.reshape(N_CHIP, 1, text_block, width)
    first = core == 0
    text_row_gradient = jnp.concatenate(
        (jnp.where(first, own_cut, other_cut), jnp.where(first, other_cut, own_cut)), axis=1
    ).reshape(text.shape)

    image_back = t_dot(order, image_back).astype(bf16)
    half = N_TENANT * PAD // 2
    image_back = jnp.concatenate((image_back[:half], image_back[half:]), axis=1)
    up_part = ADAPTER_SCALE * (t_dot(image_cot, image_low) + t_dot(text_cot, text_low))
    up_rows = value_width // (2 * N_CHIP)
    up_part = up_part.astype(bf16).reshape(N_CHIP, 2, up_rows, rank)
    up_part = jnp.concatenate((up_part[:, 0], up_part[:, 1]), axis=2)
    last = jnp.concatenate(
        (jnp.broadcast_to(image_back[None], (N_CHIP,) + image_back.shape), up_part), axis=1
    )
    last = exchange(last, CHIPS)
    up_sum = jnp.sum(last[:, half:].astype(f32), axis=0)
    up_cut = jnp.stack((up_sum[:, :rank], up_sum[:, rank:]))
    up_own = lax.dynamic_index_in_dim(up_cut, core, 0, False)
    up_other = swap(lax.dynamic_index_in_dim(up_cut, 1 - core, 0, False))
    up_matrix_gradient = (up_own + up_other).T

    backs = last[:, :half].reshape(N_CHIP, N_TENANT // 2, PAD, 2, rank)
    backs = backs.transpose(3, 1, 0, 2, 4).reshape(N_TENANT * N_CHIP * PAD, rank)
    visual_all = visual_all.reshape(N_TENANT * N_CHIP * PAD, 2 * width)
    text_backs = text_back_rows[:, value_width:]
    down_parts = t_dot(visual_all, backs)
    down_own = down_parts[:width] + t_dot(text_own, text_backs)
    down_send = down_parts[width:] + t_dot(text_other, text_backs)
    down_gradient = down_own + swap(down_send)
    return (values[None], down_gradient[None], up_matrix_gradient[None], text_row_gradient[None])


def solution(mesh):
    fine = Mesh(mesh.devices.reshape(8, 2, 2, 8, 2), TENANT + FSDP)
    in_specs = (
        P(TENANT + FSDP, None),
        P(),
        P(None, FSDP),
        P(FSDP, None),
        P(TENANT, FSDP, None),
        P(TENANT, None, None),
        P(TENANT, None, FSDP),
        P(TENANT, None),
        P(TENANT, FSDP, None),
        P(TENANT, FSDP),
    )
    out_specs = (
        P(TENANT, FSDP, None),
        P(TENANT, FSDP, None),
        P(TENANT, None, FSDP),
        P(TENANT, None, FSDP),
    )
    return jax.shard_map(body, mesh=fine, in_specs=in_specs, out_specs=out_specs, check_vma=False)
```

```python
import jax
import jax.numpy as jnp
from jax import lax
from jax.sharding import Mesh, PartitionSpec as P

ADAPTER_SCALE = 0.5
TENANT = ("y", "x_lo")
CHIPS = ("x_hi", "z")
FSDP = ("x_hi", "z", "core")
N_CHIP = 16
N_Z = 8
N_TENANT = 16
PAD = 8


def swap(block, axis="core"):
    return lax.ppermute(block, axis, [(0, 1), (1, 0)])


def pick(block, axis, index):
    return lax.dynamic_index_in_dim(block, index, axis, False)


def by_place(place, mine, theirs, axis):
    first = place == 0
    low, high = jnp.where(first, mine, theirs), jnp.where(first, theirs, mine)
    return jnp.concatenate((low, high), axis=axis)


def exchange(block, axes):
    return lax.all_to_all(block, axes, 0, 0, tiled=True)


def share(block, axes, count):
    return exchange(jnp.broadcast_to(block[None], (count,) + block.shape), axes)


def dot(a, b):
    return jnp.dot(a, b, preferred_element_type=jnp.float32)


def dot_t(a, b):
    return lax.dot_general(a, b, (((1,), (1,)), ((), ())), preferred_element_type=jnp.float32)


def t_dot(a, b):
    return lax.dot_general(a, b, (((0,), (0,)), ((), ())), preferred_element_type=jnp.float32)


def body(
    encoded,
    encoder_norm_gain,
    encoder_projection_weight,
    frozen_value_weight,
    tenant_down_weight,
    tenant_up_weight,
    embedded_text_rows,
    image_row_index,
    targets,
    row_loss_mask,
):
    bf16, f32 = jnp.bfloat16, jnp.float32
    core = lax.axis_index("core")
    x_hi = lax.axis_index("x_hi")
    x_lo = lax.axis_index("x_lo")
    device_row = lax.axis_index(FSDP)
    down = tenant_down_weight[0]
    up = tenant_up_weight[0]
    text = embedded_text_rows[0]
    vis_dev = encoded.shape[0]
    width = text.shape[1]
    value_width = frozen_value_weight.shape[1]
    rank = down.shape[1]
    block_rows = targets.shape[1]
    text_block = text.shape[0] // (2 * N_CHIP)
    vis_block = block_rows - text_block

    features = encoded.astype(f32)
    centred = features - jnp.mean(features, axis=-1, keepdims=True)
    spread = jnp.mean(centred * centred, axis=-1, keepdims=True)
    normed = (centred * lax.rsqrt(spread + 1e-06) * encoder_norm_gain.astype(f32)).astype(bf16)
    normed = jnp.pad(normed, ((0, PAD - vis_dev), (0, 0)))
    normed_rows = share(normed, CHIPS, N_CHIP).reshape(N_CHIP * PAD, -1)

    text_cut = text.reshape(2, N_Z, 2, text_block, width)
    text_own = pick(text_cut, 2, core).transpose(1, 0, 2, 3).reshape(-1, width)
    text_send = pick(text_cut, 2, 1 - core).transpose(1, 0, 2, 3).reshape(-1, width)
    text_other = swap(text_send)
    mixed_own = jnp.concatenate((frozen_value_weight, down), axis=1)
    mixed_other = swap(mixed_own)
    wanted, mask = targets[0], row_loss_mask[0]
    text_mask = jnp.broadcast_to(mask[vis_block:, None].astype(bf16), (text_block, 128))
    text_wanted = jnp.concatenate((wanted[vis_block:], text_mask), axis=1)
    text_wanted = by_place(x_hi, text_wanted, swap(text_wanted, "x_hi"), 0)
    projection_other = swap(encoder_projection_weight)
    down_pair = jnp.concatenate((down, mixed_other[:, value_width:]), axis=0)
    down_pair = by_place(x_lo, down_pair, swap(down_pair, "x_lo"), 1)
    all_down = lax.all_gather(down_pair, "y", axis=0)
    all_down = all_down.transpose(1, 0, 2).reshape(2 * width, N_TENANT * rank)

    text_part = (dot(text_own, mixed_own) + dot(text_other, mixed_other)).astype(bf16)
    text_parts = lax.psum_scatter(text_part, "z", scatter_dimension=0, tiled=True)

    projection = jnp.concatenate((encoder_projection_weight, projection_other), axis=1)
    visual = jax.nn.gelu(dot(normed_rows, projection)).astype(bf16)
    frozen_weight = jnp.concatenate((frozen_value_weight, mixed_other[:, :value_width]), axis=0)
    image_part = jnp.concatenate(
        (dot(visual, frozen_weight).astype(bf16), dot(visual, all_down).astype(bf16)), axis=1
    )
    image_parts = exchange(image_part.reshape(N_CHIP, PAD, -1), CHIPS)
    image_sum = jnp.sum(image_parts.astype(f32), axis=0).astype(bf16)
    image_low = image_sum[:, value_width:].reshape(PAD, N_TENANT, rank).transpose(1, 0, 2)
    image_frozen = jnp.broadcast_to(image_sum[None, :, :value_width], (N_TENANT, PAD, value_width))
    image_send = jnp.concatenate((image_frozen, image_low), axis=2)
    text_parts, image_send = lax.optimization_barrier((text_parts, image_send))
    image_rows = exchange(image_send, TENANT)
    text_sum = (text_parts.astype(f32) + swap(text_parts, "x_hi").astype(f32)).astype(bf16)
    visual_pair = by_place(x_lo, visual, swap(visual, "x_lo"), 0)
    visual_all = lax.all_gather(visual_pair, "y", axis=0, tiled=True)

    place = lax.dynamic_slice_in_dim(image_row_index[0], device_row * vis_block, vis_block, 0)
    group = place // (2 * N_CHIP * vis_dev)
    slot = place - group * (2 * N_CHIP * vis_dev) - device_row * vis_dev
    order = (group * PAD + slot)[:, None] == jnp.arange(N_TENANT * PAD, dtype=jnp.int32)[None]
    order = order.astype(bf16)
    image_rows = image_rows.reshape(N_TENANT * PAD, value_width + rank)
    picked = dot(order, image_rows).astype(bf16)

    def rows_of(block, wanted, mask):
        frozen, low = block[:, :value_width], block[:, value_width:]
        mixed = frozen.astype(f32) + ADAPTER_SCALE * dot(low, up)
        values = mixed.astype(bf16)
        weight = mask.astype(f32)[:, None]
        cotangent = (weight * (values.astype(f32) - wanted.astype(f32)) * 0.25).astype(bf16)
        back = (ADAPTER_SCALE * dot_t(cotangent, up).astype(bf16).astype(f32)).astype(bf16)
        return low, values, cotangent, back

    text_low, text_values, text_cot, text_back = rows_of(
        text_sum, text_wanted[:, :value_width], text_wanted[:, value_width]
    )
    text_back_rows = jnp.concatenate((text_cot, text_back), axis=1)
    text_back_rows = lax.all_gather(text_back_rows, "z", axis=0, tiled=True)
    own_text = (text_low, text_values, text_cot)
    text_low, text_values, text_cot = (
        pick(r.reshape(2, text_block, -1), 0, x_hi) for r in own_text
    )
    image_low, image_values, image_cot, image_back = rows_of(
        picked, wanted[:vis_block], mask[:vis_block]
    )
    values = jnp.concatenate((image_values, text_values), axis=0)

    text_grad_own = dot_t(text_back_rows, mixed_own).astype(bf16)
    text_grad_send = dot_t(text_back_rows, mixed_other).astype(bf16)
    text_grad_other = swap(text_grad_send)
    cut = (N_Z, 2, 1, text_block, width)
    text_row_gradient = by_place(core, text_grad_own.reshape(cut), text_grad_other.reshape(cut), 2)
    text_row_gradient = text_row_gradient.transpose(1, 0, 2, 3, 4).reshape(text.shape)

    image_back = t_dot(order, image_back).astype(bf16)
    half = N_TENANT * PAD // 2
    image_back = jnp.concatenate((image_back[:half], image_back[half:]), axis=1)
    up_part = ADAPTER_SCALE * (t_dot(image_cot, image_low) + t_dot(text_cot, text_low))
    up_rows = value_width // (2 * N_CHIP)
    up_part = up_part.astype(bf16).reshape(N_CHIP, 2, up_rows, rank)
    up_part = jnp.concatenate((up_part[:, 0], up_part[:, 1]), axis=2)
    last = jnp.concatenate(
        (jnp.broadcast_to(image_back[None], (N_CHIP,) + image_back.shape), up_part), axis=1
    )
    last = exchange(last, CHIPS)
    up_sum = jnp.sum(last[:, half:].astype(f32), axis=0)
    up_cut = jnp.stack((up_sum[:, :rank], up_sum[:, rank:]))
    up_own = lax.dynamic_index_in_dim(up_cut, core, 0, False)
    up_other = swap(lax.dynamic_index_in_dim(up_cut, 1 - core, 0, False))
    up_matrix_gradient = (up_own + up_other).T

    backs = last[:, :half].reshape(N_CHIP, N_TENANT // 2, PAD, 2, rank)
    backs = backs.transpose(3, 1, 0, 2, 4).reshape(N_TENANT * N_CHIP * PAD, rank)
    text_backs = text_back_rows[:, value_width:]
    down_parts = t_dot(visual_all, backs)
    down_own = down_parts[:width] + t_dot(text_own, text_backs)
    down_send = down_parts[width:] + t_dot(text_other, text_backs)
    down_gradient = down_own + swap(down_send)
    return (values[None], down_gradient[None], up_matrix_gradient[None], text_row_gradient[None])


def solution(mesh):
    fine = Mesh(mesh.devices.reshape(8, 2, 2, 8, 2), TENANT + FSDP)
    in_specs = (
        P(TENANT + FSDP, None),
        P(),
        P(None, FSDP),
        P(FSDP, None),
        P(TENANT, FSDP, None),
        P(TENANT, None, None),
        P(TENANT, None, FSDP),
        P(TENANT, None),
        P(TENANT, FSDP, None),
        P(TENANT, FSDP),
    )
    out_specs = (
        P(TENANT, FSDP, None),
        P(TENANT, FSDP, None),
        P(TENANT, None, FSDP),
        P(TENANT, None, FSDP),
    )
    return jax.shard_map(body, mesh=fine, in_specs=in_specs, out_specs=out_specs, check_vma=False)
```

```python
import jax
import jax.numpy as jnp
from jax import lax
from jax.sharding import Mesh, PartitionSpec as P

ADAPTER_SCALE = 0.5
TENANT = ("y", "x_lo")
CHIPS = ("x_hi", "z")
FSDP = ("x_hi", "z", "core")
N_CHIP = 16
N_Z = 8
N_TENANT = 16
PAD = 8


def swap(block, axis="core"):
    return lax.ppermute(block, axis, [(0, 1), (1, 0)])


def pick(block, axis, index):
    return lax.dynamic_index_in_dim(block, index, axis, False)


def by_place(place, mine, theirs, axis):
    first = place == 0
    low, high = jnp.where(first, mine, theirs), jnp.where(first, theirs, mine)
    return jnp.concatenate((low, high), axis=axis)


def exchange(block, axes):
    return lax.all_to_all(block, axes, 0, 0, tiled=True)


def share(block, axes, count):
    return exchange(jnp.broadcast_to(block[None], (count,) + block.shape), axes)


def dot(a, b):
    return jnp.dot(a, b, preferred_element_type=jnp.float32)


def dot_t(a, b):
    return lax.dot_general(a, b, (((1,), (1,)), ((), ())), preferred_element_type=jnp.float32)


def t_dot(a, b):
    return lax.dot_general(a, b, (((0,), (0,)), ((), ())), preferred_element_type=jnp.float32)


def body(
    encoded,
    encoder_norm_gain,
    encoder_projection_weight,
    frozen_value_weight,
    tenant_down_weight,
    tenant_up_weight,
    embedded_text_rows,
    image_row_index,
    targets,
    row_loss_mask,
):
    bf16, f32 = jnp.bfloat16, jnp.float32
    core = lax.axis_index("core")
    x_hi = lax.axis_index("x_hi")
    x_lo = lax.axis_index("x_lo")
    device_row = lax.axis_index(FSDP)
    down = tenant_down_weight[0]
    up = tenant_up_weight[0]
    text = embedded_text_rows[0]
    vis_dev = encoded.shape[0]
    width = text.shape[1]
    value_width = frozen_value_weight.shape[1]
    rank = down.shape[1]
    block_rows = targets.shape[1]
    text_block = text.shape[0] // (2 * N_CHIP)
    vis_block = block_rows - text_block

    features = encoded.astype(f32)
    centred = features - jnp.mean(features, axis=-1, keepdims=True)
    spread = jnp.mean(centred * centred, axis=-1, keepdims=True)
    normed = (centred * lax.rsqrt(spread + 1e-06) * encoder_norm_gain.astype(f32)).astype(bf16)
    normed = jnp.pad(normed, ((0, PAD - vis_dev), (0, 0)))
    normed_rows = share(normed, CHIPS, N_CHIP).reshape(N_CHIP * PAD, -1)

    text_cut = text.reshape(2, N_Z, 2, text_block, width)
    text_own = pick(text_cut, 2, core).transpose(1, 0, 2, 3).reshape(-1, width)
    text_send = pick(text_cut, 2, 1 - core).transpose(1, 0, 2, 3).reshape(-1, width)
    text_other = swap(text_send)
    mixed_own = jnp.concatenate((frozen_value_weight, down), axis=1)
    mixed_other = swap(mixed_own)
    wanted, mask = targets[0], row_loss_mask[0]
    text_mask = jnp.broadcast_to(mask[vis_block:, None].astype(bf16), (text_block, 128))
    text_wanted = jnp.concatenate((wanted[vis_block:], text_mask), axis=1)
    text_wanted = by_place(x_hi, text_wanted, swap(text_wanted, "x_hi"), 0)
    projection_other = swap(encoder_projection_weight)
    down_wide = jnp.concatenate((down.T, mixed_other[:, value_width:].T), axis=1)
    down_pair = by_place(x_lo, down_wide, swap(down_wide, "x_lo"), 0)
    all_down = lax.all_gather(down_pair, "y", axis=0, tiled=True)

    text_part = (dot(text_own, mixed_own) + dot(text_other, mixed_other)).astype(bf16)
    text_parts = lax.psum_scatter(text_part, "z", scatter_dimension=0, tiled=True)

    projection = jnp.concatenate((encoder_projection_weight, projection_other), axis=1)
    visual = jax.nn.gelu(dot(normed_rows, projection)).astype(bf16)
    frozen_weight = jnp.concatenate((frozen_value_weight, mixed_other[:, :value_width]), axis=0)
    image_part = jnp.concatenate(
        (dot(visual, frozen_weight).astype(bf16), dot_t(visual, all_down).astype(bf16)), axis=1
    )
    image_parts = exchange(image_part.reshape(N_CHIP, PAD, -1), CHIPS)
    image_sum = jnp.sum(image_parts.astype(f32), axis=0).astype(bf16)
    text_parts, image_sum = lax.optimization_barrier((text_parts, image_sum))
    text_sum = (text_parts.astype(f32) + swap(text_parts, "x_hi").astype(f32)).astype(bf16)
    image_low = image_sum[:, value_width:].reshape(PAD, N_TENANT, rank).transpose(1, 0, 2)
    image_frozen = jnp.broadcast_to(image_sum[None, :, :value_width], (N_TENANT, PAD, value_width))
    image_send = jnp.concatenate((image_frozen, image_low), axis=2)
    image_rows = exchange(image_send, TENANT)
    visual_rows = visual.reshape(N_CHIP, PAD, 2 * width)[:, :vis_dev].reshape(-1, 2 * width)
    visual_pair = by_place(x_lo, visual_rows, swap(visual_rows, "x_lo"), 0)
    visual_all = lax.all_gather(visual_pair, "y", axis=0, tiled=True)

    place = lax.dynamic_slice_in_dim(image_row_index[0], device_row * vis_block, vis_block, 0)
    group = place // (2 * N_CHIP * vis_dev)
    slot = place - group * (2 * N_CHIP * vis_dev) - device_row * vis_dev
    order = (group * PAD + slot)[:, None] == jnp.arange(N_TENANT * PAD, dtype=jnp.int32)[None]
    order = order.astype(bf16)
    image_rows = image_rows.reshape(N_TENANT * PAD, value_width + rank)
    picked = dot(order, image_rows).astype(bf16)

    def rows_of(block, wanted, mask):
        frozen, low = block[:, :value_width], block[:, value_width:]
        mixed = frozen.astype(f32) + ADAPTER_SCALE * dot(low, up)
        values = mixed.astype(bf16)
        weight = mask.astype(f32)[:, None]
        cotangent = (weight * (values.astype(f32) - wanted.astype(f32)) * 0.25).astype(bf16)
        back = (ADAPTER_SCALE * dot_t(cotangent, up).astype(bf16).astype(f32)).astype(bf16)
        return low, values, cotangent, back

    text_low, text_values, text_cot, text_back = rows_of(
        text_sum, text_wanted[:, :value_width], text_wanted[:, value_width]
    )
    text_back_rows = jnp.concatenate((text_cot, text_back), axis=1)
    text_back_rows = lax.all_gather(text_back_rows, "z", axis=0, tiled=True)
    own_text = (text_low, text_values, text_cot)
    text_low, text_values, text_cot = (
        pick(r.reshape(2, text_block, -1), 0, x_hi) for r in own_text
    )
    image_low, image_values, image_cot, image_back = rows_of(
        picked, wanted[:vis_block], mask[:vis_block]
    )
    values = jnp.concatenate((image_values, text_values), axis=0)

    text_grad_own = dot_t(text_back_rows, mixed_own).astype(bf16)
    text_grad_send = dot_t(text_back_rows, mixed_other).astype(bf16)
    text_grad_other = swap(text_grad_send)
    cut = (N_Z, 2, 1, text_block, width)
    text_row_gradient = by_place(core, text_grad_own.reshape(cut), text_grad_other.reshape(cut), 2)
    text_row_gradient = text_row_gradient.transpose(1, 0, 2, 3, 4).reshape(text.shape)

    image_back = t_dot(order, image_back).astype(bf16)
    half = N_TENANT * PAD // 2
    image_back = jnp.concatenate((image_back[:half], image_back[half:]), axis=1)
    up_part = ADAPTER_SCALE * (t_dot(image_cot, image_low) + t_dot(text_cot, text_low))
    up_rows = value_width // (2 * N_CHIP)
    up_part = up_part.astype(bf16).reshape(N_CHIP, 2, up_rows, rank)
    up_part = jnp.concatenate((up_part[:, 0], up_part[:, 1]), axis=2)
    last = jnp.concatenate(
        (jnp.broadcast_to(image_back[None], (N_CHIP,) + image_back.shape), up_part), axis=1
    )
    last = exchange(last, CHIPS)
    up_sum = jnp.sum(last[:, half:].astype(f32), axis=0)
    up_cut = jnp.stack((up_sum[:, :rank], up_sum[:, rank:]))
    up_own = lax.dynamic_index_in_dim(up_cut, core, 0, False)
    up_other = swap(lax.dynamic_index_in_dim(up_cut, 1 - core, 0, False))
    up_matrix_gradient = (up_own + up_other).T

    backs = last[:, :half].reshape(N_CHIP, N_TENANT // 2, PAD, 2, rank)[:, :, :vis_dev]
    backs = backs.transpose(3, 1, 0, 2, 4).reshape(N_TENANT * N_CHIP * vis_dev, rank)
    text_backs = text_back_rows[:, value_width:]
    down_parts = t_dot(visual_all, backs)
    down_own = down_parts[:width] + t_dot(text_own, text_backs)
    down_send = down_parts[width:] + t_dot(text_other, text_backs)
    down_gradient = down_own + swap(down_send)
    return (values[None], down_gradient[None], up_matrix_gradient[None], text_row_gradient[None])


def solution(mesh):
    fine = Mesh(mesh.devices.reshape(8, 2, 2, 8, 2), TENANT + FSDP)
    in_specs = (
        P(TENANT + FSDP, None),
        P(),
        P(None, FSDP),
        P(FSDP, None),
        P(TENANT, FSDP, None),
        P(TENANT, None, None),
        P(TENANT, None, FSDP),
        P(TENANT, None),
        P(TENANT, FSDP, None),
        P(TENANT, FSDP),
    )
    out_specs = (
        P(TENANT, FSDP, None),
        P(TENANT, FSDP, None),
        P(TENANT, None, FSDP),
        P(TENANT, None, FSDP),
    )
    return jax.shard_map(body, mesh=fine, in_specs=in_specs, out_specs=out_specs, check_vma=False)
```

```python
import jax
import jax.numpy as jnp
from jax import lax
from jax.sharding import Mesh, PartitionSpec as P

ADAPTER_SCALE = 0.5
TENANT = ("y", "x_lo")
CHIPS = ("x_hi", "z")
FSDP = ("x_hi", "z", "core")
N_CHIP = 16
N_Z = 8
N_TENANT = 16
PAD = 8


def swap(block, axis="core"):
    return lax.ppermute(block, axis, [(0, 1), (1, 0)])


def pick(block, axis, index):
    return lax.dynamic_index_in_dim(block, index, axis, False)


def by_place(place, mine, theirs, axis):
    first = place == 0
    low, high = jnp.where(first, mine, theirs), jnp.where(first, theirs, mine)
    return jnp.concatenate((low, high), axis=axis)


def exchange(block, axes):
    return lax.all_to_all(block, axes, 0, 0, tiled=True)


def share(block, axes, count):
    return exchange(jnp.broadcast_to(block[None], (count,) + block.shape), axes)


def dot(a, b):
    return jnp.dot(a, b, preferred_element_type=jnp.float32)


def dot_t(a, b):
    return lax.dot_general(a, b, (((1,), (1,)), ((), ())), preferred_element_type=jnp.float32)


def t_dot(a, b):
    return lax.dot_general(a, b, (((0,), (0,)), ((), ())), preferred_element_type=jnp.float32)


def body(
    encoded,
    encoder_norm_gain,
    encoder_projection_weight,
    frozen_value_weight,
    tenant_down_weight,
    tenant_up_weight,
    embedded_text_rows,
    image_row_index,
    targets,
    row_loss_mask,
):
    bf16, f32 = jnp.bfloat16, jnp.float32
    core = lax.axis_index("core")
    x_hi = lax.axis_index("x_hi")
    x_lo = lax.axis_index("x_lo")
    device_row = lax.axis_index(FSDP)
    down = tenant_down_weight[0]
    up = tenant_up_weight[0]
    text = embedded_text_rows[0]
    vis_dev = encoded.shape[0]
    width = text.shape[1]
    value_width = frozen_value_weight.shape[1]
    rank = down.shape[1]
    block_rows = targets.shape[1]
    text_block = text.shape[0] // (2 * N_CHIP)
    vis_block = block_rows - text_block

    features = encoded.astype(f32)
    centred = features - jnp.mean(features, axis=-1, keepdims=True)
    spread = jnp.mean(centred * centred, axis=-1, keepdims=True)
    normed = (centred * lax.rsqrt(spread + 1e-06) * encoder_norm_gain.astype(f32)).astype(bf16)
    normed = jnp.pad(normed, ((0, PAD - vis_dev), (0, 0)))
    normed_rows = share(normed, CHIPS, N_CHIP).reshape(N_CHIP * PAD, -1)

    text_cut = text.reshape(2, N_Z, 2, text_block, width)
    text_own = pick(text_cut, 2, core).transpose(1, 0, 2, 3).reshape(-1, width)
    text_send = pick(text_cut, 2, 1 - core).transpose(1, 0, 2, 3).reshape(-1, width)
    mixed_own = jnp.concatenate((frozen_value_weight, down), axis=1)
    down_other = swap(down)
    down_wide = jnp.concatenate((down.T, down_other.T), axis=1)
    down_pair = by_place(x_lo, down_wide, swap(down_wide, "x_lo"), 0)
    text_send, frozen_send, projection_send, down_pair = lax.optimization_barrier(
        (text_send, frozen_value_weight, encoder_projection_weight, down_pair)
    )
    all_down = lax.all_gather(down_pair, "y", axis=0, tiled=True)
    text_other = swap(text_send)
    frozen_other = swap(frozen_send)
    mixed_other = jnp.concatenate((frozen_other, down_other), axis=1)
    wanted, mask = targets[0], row_loss_mask[0]
    text_mask = jnp.broadcast_to(mask[vis_block:, None].astype(bf16), (text_block, 128))
    text_wanted = jnp.concatenate((wanted[vis_block:], text_mask), axis=1)
    text_wanted = by_place(x_hi, text_wanted, swap(text_wanted, "x_hi"), 0)
    projection_other = swap(projection_send)
    text_part = (dot(text_own, mixed_own) + dot(text_other, mixed_other)).astype(bf16)
    text_parts = lax.psum_scatter(text_part, "z", scatter_dimension=0, tiled=True)

    projection = jnp.concatenate((encoder_projection_weight, projection_other), axis=1)
    visual = jax.nn.gelu(dot(normed_rows, projection)).astype(bf16)
    frozen_weight = jnp.concatenate((frozen_value_weight, frozen_other), axis=0)
    image_part = jnp.concatenate(
        (dot(visual, frozen_weight).astype(bf16), dot_t(visual, all_down).astype(bf16)), axis=1
    )
    image_parts = exchange(image_part.reshape(N_CHIP, PAD, -1), CHIPS)
    image_sum = jnp.sum(image_parts.astype(f32), axis=0).astype(bf16)
    text_parts, image_sum = lax.optimization_barrier((text_parts, image_sum))
    text_sum = (text_parts.astype(f32) + swap(text_parts, "x_hi").astype(f32)).astype(bf16)
    image_low = image_sum[:, value_width:].reshape(PAD, N_TENANT, rank).transpose(1, 0, 2)
    image_frozen = jnp.broadcast_to(image_sum[None, :, :value_width], (N_TENANT, PAD, value_width))
    image_send = jnp.concatenate((image_frozen, image_low), axis=2)
    image_rows = exchange(image_send, TENANT)
    visual_rows = visual.reshape(N_CHIP, PAD, 2 * width)[:, :vis_dev].reshape(-1, 2 * width)
    visual_pair = by_place(x_lo, visual_rows, swap(visual_rows, "x_lo"), 0)
    visual_all = lax.all_gather(visual_pair, "y", axis=0, tiled=True)

    place = lax.dynamic_slice_in_dim(image_row_index[0], device_row * vis_block, vis_block, 0)
    group = place // (2 * N_CHIP * vis_dev)
    slot = place - group * (2 * N_CHIP * vis_dev) - device_row * vis_dev
    order = (group * PAD + slot)[:, None] == jnp.arange(N_TENANT * PAD, dtype=jnp.int32)[None]
    order = order.astype(bf16)
    image_rows = image_rows.reshape(N_TENANT * PAD, value_width + rank)
    picked = dot(order, image_rows).astype(bf16)

    def rows_of(block, wanted, mask):
        frozen, low = block[:, :value_width], block[:, value_width:]
        mixed = frozen.astype(f32) + ADAPTER_SCALE * dot(low, up)
        values = mixed.astype(bf16)
        weight = mask.astype(f32)[:, None]
        cotangent = (weight * (values.astype(f32) - wanted.astype(f32)) * 0.25).astype(bf16)
        back = (ADAPTER_SCALE * dot_t(cotangent, up).astype(bf16).astype(f32)).astype(bf16)
        return low, values, cotangent, back

    text_low, text_values, text_cot, text_back = rows_of(
        text_sum, text_wanted[:, :value_width], text_wanted[:, value_width]
    )
    text_back_rows = jnp.concatenate((text_cot, text_back), axis=1)
    text_back_rows = lax.all_gather(text_back_rows, "z", axis=0, tiled=True)
    own_text = (text_low, text_values, text_cot)
    text_low, text_values, text_cot = (
        pick(r.reshape(2, text_block, -1), 0, x_hi) for r in own_text
    )
    image_low, image_values, image_cot, image_back = rows_of(
        picked, wanted[:vis_block], mask[:vis_block]
    )
    values = jnp.concatenate((image_values, text_values), axis=0)

    text_grad_own = dot_t(text_back_rows, mixed_own).astype(bf16)
    text_grad_send = dot_t(text_back_rows, mixed_other).astype(bf16)
    text_grad_other = swap(text_grad_send)
    cut = (N_Z, 2, 1, text_block, width)
    text_row_gradient = by_place(core, text_grad_own.reshape(cut), text_grad_other.reshape(cut), 2)
    text_row_gradient = text_row_gradient.transpose(1, 0, 2, 3, 4).reshape(text.shape)

    image_back = t_dot(order, image_back).astype(bf16)
    half = N_TENANT * PAD // 2
    image_back = jnp.concatenate((image_back[:half], image_back[half:]), axis=1)
    up_part = ADAPTER_SCALE * (t_dot(image_cot, image_low) + t_dot(text_cot, text_low))
    up_rows = value_width // (2 * N_CHIP)
    up_part = up_part.astype(bf16).reshape(N_CHIP, 2, up_rows, rank)
    up_part = jnp.concatenate((up_part[:, 0], up_part[:, 1]), axis=2)
    last = jnp.concatenate(
        (jnp.broadcast_to(image_back[None], (N_CHIP,) + image_back.shape), up_part), axis=1
    )
    last = exchange(last, CHIPS)
    up_sum = jnp.sum(last[:, half:].astype(f32), axis=0)
    up_cut = jnp.stack((up_sum[:, :rank], up_sum[:, rank:]))
    up_own = lax.dynamic_index_in_dim(up_cut, core, 0, False)
    up_other = swap(lax.dynamic_index_in_dim(up_cut, 1 - core, 0, False))
    up_matrix_gradient = (up_own + up_other).T

    backs = last[:, :half].reshape(N_CHIP, N_TENANT // 2, PAD, 2, rank)[:, :, :vis_dev]
    backs = backs.transpose(3, 1, 0, 2, 4).reshape(N_TENANT * N_CHIP * vis_dev, rank)
    text_backs = text_back_rows[:, value_width:]
    down_parts = t_dot(visual_all, backs)
    down_own = down_parts[:width] + t_dot(text_own, text_backs)
    down_send = down_parts[width:] + t_dot(text_other, text_backs)
    down_gradient = down_own + swap(down_send)
    return (values[None], down_gradient[None], up_matrix_gradient[None], text_row_gradient[None])


def solution(mesh):
    fine = Mesh(mesh.devices.reshape(8, 2, 2, 8, 2), TENANT + FSDP)
    in_specs = (
        P(TENANT + FSDP, None),
        P(),
        P(None, FSDP),
        P(FSDP, None),
        P(TENANT, FSDP, None),
        P(TENANT, None, None),
        P(TENANT, None, FSDP),
        P(TENANT, None),
        P(TENANT, FSDP, None),
        P(TENANT, FSDP),
    )
    out_specs = (
        P(TENANT, FSDP, None),
        P(TENANT, FSDP, None),
        P(TENANT, None, FSDP),
        P(TENANT, None, FSDP),
    )
    return jax.shard_map(body, mesh=fine, in_specs=in_specs, out_specs=out_specs, check_vma=False)
```

```python
import jax
import jax.numpy as jnp
from jax import lax
from jax.sharding import Mesh, PartitionSpec as P

ADAPTER_SCALE = 0.5
TENANT = ("y", "x_lo")
CHIPS = ("x_hi", "z")
FSDP = ("x_hi", "z", "core")
N_CHIP = 16
N_Z = 8
N_TENANT = 16
PAD = 8


def swap(block, axis="core"):
    return lax.ppermute(block, axis, [(0, 1), (1, 0)])


def pick(block, axis, index):
    return lax.dynamic_index_in_dim(block, index, axis, False)


def by_place(place, mine, theirs, axis):
    first = place == 0
    low, high = jnp.where(first, mine, theirs), jnp.where(first, theirs, mine)
    return jnp.concatenate((low, high), axis=axis)


def exchange(block, axes):
    return lax.all_to_all(block, axes, 0, 0, tiled=True)


def share(block, axes, count):
    return exchange(jnp.broadcast_to(block[None], (count,) + block.shape), axes)


def dot(a, b):
    return jnp.dot(a, b, preferred_element_type=jnp.float32)


def dot_t(a, b):
    return lax.dot_general(a, b, (((1,), (1,)), ((), ())), preferred_element_type=jnp.float32)


def t_dot(a, b):
    return lax.dot_general(a, b, (((0,), (0,)), ((), ())), preferred_element_type=jnp.float32)


def body(
    encoded,
    encoder_norm_gain,
    encoder_projection_weight,
    frozen_value_weight,
    tenant_down_weight,
    tenant_up_weight,
    embedded_text_rows,
    image_row_index,
    targets,
    row_loss_mask,
):
    bf16, f32 = jnp.bfloat16, jnp.float32
    core = lax.axis_index("core")
    x_hi = lax.axis_index("x_hi")
    x_lo = lax.axis_index("x_lo")
    device_row = lax.axis_index(FSDP)
    down = tenant_down_weight[0]
    up = tenant_up_weight[0]
    text = embedded_text_rows[0]
    vis_dev = encoded.shape[0]
    width = text.shape[1]
    value_width = frozen_value_weight.shape[1]
    rank = down.shape[1]
    block_rows = targets.shape[1]
    text_block = text.shape[0] // (2 * N_CHIP)
    vis_block = block_rows - text_block

    features = encoded.astype(f32)
    centred = features - jnp.mean(features, axis=-1, keepdims=True)
    spread = jnp.mean(centred * centred, axis=-1, keepdims=True)
    normed = (centred * lax.rsqrt(spread + 1e-06) * encoder_norm_gain.astype(f32)).astype(bf16)
    normed = jnp.pad(normed, ((0, PAD - vis_dev), (0, 0)))
    normed_rows = share(normed, CHIPS, N_CHIP).reshape(N_CHIP * PAD, -1)

    text_cut = text.reshape(2, N_Z, 2, text_block, width)
    text_own = pick(text_cut, 2, core).transpose(1, 0, 2, 3).reshape(-1, width)
    text_send = pick(text_cut, 2, 1 - core).transpose(1, 0, 2, 3).reshape(-1, width)
    mixed_own = jnp.concatenate((frozen_value_weight, down), axis=1)
    down_other = swap(down)
    down_wide = jnp.concatenate((down.T, down_other.T), axis=1)
    down_pair = by_place(x_lo, down_wide, swap(down_wide, "x_lo"), 0)
    text_send, frozen_send, projection_send, down_pair = lax.optimization_barrier(
        (text_send, frozen_value_weight, encoder_projection_weight, down_pair)
    )
    all_down = lax.all_gather(down_pair, "y", axis=0, tiled=True)
    text_other = swap(text_send)
    frozen_other = swap(frozen_send)
    mixed_other = jnp.concatenate((frozen_other, down_other), axis=1)
    wanted, mask = targets[0], row_loss_mask[0]
    text_mask = jnp.broadcast_to(mask[vis_block:, None].astype(bf16), (text_block, 128))
    text_wanted = jnp.concatenate((wanted[vis_block:], text_mask), axis=1)
    text_wanted = by_place(x_hi, text_wanted, swap(text_wanted, "x_hi"), 0)
    projection_other = swap(projection_send)
    text_part = (dot(text_own, mixed_own) + dot(text_other, mixed_other)).astype(bf16)
    text_parts = lax.psum_scatter(text_part, "z", scatter_dimension=0, tiled=True)

    projection = jnp.concatenate((encoder_projection_weight, projection_other), axis=1)
    visual = jax.nn.gelu(dot(normed_rows, projection)).astype(bf16)
    frozen_weight = jnp.concatenate((frozen_value_weight, frozen_other), axis=0)
    image_part = jnp.concatenate(
        (dot(visual, frozen_weight).astype(bf16), dot_t(visual, all_down).astype(bf16)), axis=1
    )
    image_parts = exchange(image_part.reshape(N_CHIP, PAD, -1), CHIPS)
    image_sum = jnp.sum(image_parts.astype(f32), axis=0).astype(bf16)
    text_parts, image_sum = lax.optimization_barrier((text_parts, image_sum))
    text_sum = (text_parts.astype(f32) + swap(text_parts, "x_hi").astype(f32)).astype(bf16)
    image_low = image_sum[:, value_width:].reshape(PAD, N_TENANT, rank).transpose(1, 0, 2)
    image_frozen = jnp.broadcast_to(image_sum[None, :, :value_width], (N_TENANT, PAD, value_width))
    image_send = jnp.concatenate((image_frozen, image_low), axis=2)
    visual_rows = visual.reshape(N_CHIP, PAD, 2 * width)[:, :vis_dev].reshape(-1, 2 * width)
    visual_pair = by_place(x_lo, visual_rows, swap(visual_rows, "x_lo"), 0)
    visual_all = lax.all_gather(visual_pair, "y", axis=0, tiled=True)

    place = lax.dynamic_slice_in_dim(image_row_index[0], device_row * vis_block, vis_block, 0)
    group = place // (2 * N_CHIP * vis_dev)
    slot = place - group * (2 * N_CHIP * vis_dev) - device_row * vis_dev
    order = (group * PAD + slot)[:, None] == jnp.arange(N_TENANT * PAD, dtype=jnp.int32)[None]
    order = order.astype(bf16)

    def rows_of(block, wanted, mask):
        frozen, low = block[:, :value_width], block[:, value_width:]
        mixed = frozen.astype(f32) + ADAPTER_SCALE * dot(low, up)
        values = mixed.astype(bf16)
        weight = mask.astype(f32)[:, None]
        cotangent = (weight * (values.astype(f32) - wanted.astype(f32)) * 0.25).astype(bf16)
        back = (ADAPTER_SCALE * dot_t(cotangent, up).astype(bf16).astype(f32)).astype(bf16)
        return low, values, cotangent, back

    text_low, text_values, text_cot, text_back = rows_of(
        text_sum, text_wanted[:, :value_width], text_wanted[:, value_width]
    )
    text_back_rows = jnp.concatenate((text_cot, text_back), axis=1)
    text_back_rows, image_send = lax.optimization_barrier((text_back_rows, image_send))
    image_rows = exchange(image_send, TENANT)
    image_rows = image_rows.reshape(N_TENANT * PAD, value_width + rank)
    picked = dot(order, image_rows).astype(bf16)
    text_back_rows = lax.all_gather(text_back_rows, "z", axis=0, tiled=True)
    own_text = (text_low, text_values, text_cot)
    text_low, text_values, text_cot = (
        pick(r.reshape(2, text_block, -1), 0, x_hi) for r in own_text
    )
    image_low, image_values, image_cot, image_back = rows_of(
        picked, wanted[:vis_block], mask[:vis_block]
    )
    values = jnp.concatenate((image_values, text_values), axis=0)

    text_grad_own = dot_t(text_back_rows, mixed_own).astype(bf16)
    text_grad_send = dot_t(text_back_rows, mixed_other).astype(bf16)
    text_grad_other = swap(text_grad_send)
    cut = (N_Z, 2, 1, text_block, width)
    text_row_gradient = by_place(core, text_grad_own.reshape(cut), text_grad_other.reshape(cut), 2)
    text_row_gradient = text_row_gradient.transpose(1, 0, 2, 3, 4).reshape(text.shape)

    image_back = t_dot(order, image_back).astype(bf16)
    half = N_TENANT * PAD // 2
    image_back = jnp.concatenate((image_back[:half], image_back[half:]), axis=1)
    up_part = ADAPTER_SCALE * (t_dot(image_cot, image_low) + t_dot(text_cot, text_low))
    up_rows = value_width // (2 * N_CHIP)
    up_part = up_part.astype(bf16).reshape(N_CHIP, 2, up_rows, rank)
    up_part = jnp.concatenate((up_part[:, 0], up_part[:, 1]), axis=2)
    last = jnp.concatenate(
        (jnp.broadcast_to(image_back[None], (N_CHIP,) + image_back.shape), up_part), axis=1
    )
    last = exchange(last, CHIPS)
    up_sum = jnp.sum(last[:, half:].astype(f32), axis=0)
    up_cut = jnp.stack((up_sum[:, :rank], up_sum[:, rank:]))
    up_own = lax.dynamic_index_in_dim(up_cut, core, 0, False)
    up_other = swap(lax.dynamic_index_in_dim(up_cut, 1 - core, 0, False))
    up_matrix_gradient = (up_own + up_other).T

    backs = last[:, :half].reshape(N_CHIP, N_TENANT // 2, PAD, 2, rank)[:, :, :vis_dev]
    backs = backs.transpose(3, 1, 0, 2, 4).reshape(N_TENANT * N_CHIP * vis_dev, rank)
    text_backs = text_back_rows[:, value_width:]
    down_parts = t_dot(visual_all, backs)
    down_own = down_parts[:width] + t_dot(text_own, text_backs)
    down_send = down_parts[width:] + t_dot(text_other, text_backs)
    down_gradient = down_own + swap(down_send)
    return (values[None], down_gradient[None], up_matrix_gradient[None], text_row_gradient[None])


def solution(mesh):
    fine = Mesh(mesh.devices.reshape(8, 2, 2, 8, 2), TENANT + FSDP)
    in_specs = (
        P(TENANT + FSDP, None),
        P(),
        P(None, FSDP),
        P(FSDP, None),
        P(TENANT, FSDP, None),
        P(TENANT, None, None),
        P(TENANT, None, FSDP),
        P(TENANT, None),
        P(TENANT, FSDP, None),
        P(TENANT, FSDP),
    )
    out_specs = (
        P(TENANT, FSDP, None),
        P(TENANT, FSDP, None),
        P(TENANT, None, FSDP),
        P(TENANT, None, FSDP),
    )
    return jax.shard_map(body, mesh=fine, in_specs=in_specs, out_specs=out_specs, check_vma=False)
```
